128 devices in a mesh: row: 32 (over x, z, core), col: 4 (over y).
Axes of the slice: x: 4, y: 4, z: 4, core: 2. Of those that a mesh axis runs over, the one named last changes fastest.
Arguments:
- base_weight: bfloat16 [28672, 8192], P('row', 'col'), may hold values from -6 to 6
- stacked_down_matrices: bfloat16 [4096, 8192], P('row', 'col'), may hold values from -6 to 6
- stacked_up_matrices: bfloat16 [28672, 4096], P('row', 'col'), may hold values from -6 to 6
- ranks: int32 [64], replicated, may hold values from 1 to 64, 2304 in all
- samples: int32 [64], replicated, may hold values from 256 to 1023
Outputs:
- merged: bfloat16 [28672, 8192], P(('row', 'col'))
The draws below stay inside these ranges and needn't reach their ends.
Inputs may be any that keep to these rules, and one draw needn't show every extreme that they name: The ranks sum to 2304; the largest is exactly 64.
All inputs are finite; a program needn't handle non-finite values.
Results may differ from the reference program's by a relative error of at most 0.0038.
Values may be sent and summed in bfloat16 or wider, within the bound.
No kernel may reach another device: no remote copies, remote signals or barrier semaphores. Data moves between devices by JAX's collectives and lax.ppermute only.
A program may use at most 128 MiB of HBM per device.

```python
import math
import jax
import jax.numpy as jnp
import numpy as np
from jax import lax

D = 8192
FF = 28672
RMAX = 64
CLIENTS = 64
RPAD = 4096
RSUM = 2304
N_ROW = 32


def set_ends(array, own_key, least, top_value):
    shape = array.shape
    spot = [jax.random.randint(jax.random.fold_in(own_key, axis), (), 0, shape[axis]) for axis in range(len(shape))]
    array = array.at[tuple(spot)].set(least)
    longest = shape.index(max(shape))
    spot[longest] = (spot[longest] + 1) % shape[longest]
    return array.at[tuple(spot)].set(top_value)


def block_levels(rng, extent, pieces, low, high):
    def one(axis_at, blocks):
        heights = jax.random.uniform(jax.random.fold_in(jax.random.fold_in(rng, 6), axis_at), (blocks,), jnp.float32, low / len(pieces), high / len(pieces))
        return jnp.repeat(jnp.exp(heights), extent[axis_at] // blocks).reshape((-1,) + (1,) * (len(extent) - axis_at - 1))

    factor_of = one(*pieces[0])
    for cut in pieces[1:]:
        factor_of = factor_of * one(*cut)
    return factor_of


def length_profile(amount, total, bound, slope):
    weights = [(1 << 20) // math.isqrt(grade ** slope) + 1 for grade in range(2, amount + 1)]
    rest, given = total - bound - (amount - 1), [1] * (amount - 1)
    while rest > 0:
        movable = [i for i in range(amount - 1) if given[i] < bound]
        whole, left = sum([weights[i] for i in movable]), rest
        for i in movable:
            extra = min(bound - given[i], max(1, left * weights[i] // whole), rest)
            given[i] = given[i] + extra
            rest = rest - extra
    return np.array([bound] + given)


def ragged_sizes(rng, amount, total, most, skew):
    if amount == 2:
        one = jax.random.randint(rng, (), max(1, total - most), min(most, total - 1) + 1)
        return jnp.stack([one, total - one])
    lengths = jnp.asarray(length_profile(amount, total, most, skew), jnp.int32)
    couples = (amount - 1) // 2
    donor, taker = lengths[1:1 + 2 * couples:2], lengths[2:2 + 2 * couples:2]
    margin = jnp.minimum(donor - 1, most - taker)
    shifted = jax.random.randint(jax.random.fold_in(rng, 1), (couples,), 0, 1 << 20) % (margin + 1)
    lengths = lengths.at[1:1 + 2 * couples:2].set(donor - shifted).at[2:2 + 2 * couples:2].set(taker + shifted)
    return lengths[jax.random.permutation(jax.random.fold_in(rng, 2), amount)]


def noise(key, dims, deviation, reach, cuts=(), kind=jnp.bfloat16):
    factor_of = block_levels(key, dims, cuts, -0.22, 0.18) if cuts else 1.0
    drawn = jax.random.normal(key, dims, jnp.float32) * deviation * factor_of
    return jnp.minimum(jnp.maximum(drawn, -reach), reach).astype(kind)


def setup_inputs(seed: int = 0) -> dict:
    arg_keys = jax.random.split(jax.random.key(seed), 6)
    return {
        "base_weight": noise(arg_keys[0], (FF, D), 1.0, 6.0, ((0, 32), (1, 4))),
        "stacked_down_matrices": noise(arg_keys[1], (RPAD, D), 1.0, 6.0, ((0, 32), (1, 4))),
        "stacked_up_matrices": noise(arg_keys[2], (FF, RPAD), 1.0, 6.0, ((0, 32), (1, 4))),
        "ranks": ragged_sizes(arg_keys[3], CLIENTS, RSUM, RMAX, 2).astype(jnp.int32),
        "samples": set_ends(jax.random.randint(arg_keys[4], (CLIENTS,), 256, 1024), jax.random.fold_in(arg_keys[4], 1), 256, 1023).astype(jnp.int32),
    }


adapter_alpha_value = 8.0

def slot_scale(ranks, samples):
    counts = samples.astype(jnp.float32)
    client_weight_fraction = counts / jnp.sum(counts)
    client_scale_factor = client_weight_fraction * adapter_alpha_value / jnp.sqrt(ranks.astype(jnp.float32))
    is_live = jnp.arange(RMAX, dtype=jnp.int32)[None, :] < ranks[:, None]
    return jnp.where(is_live, client_scale_factor[:, None], jnp.float32(0.0)).reshape(-1)

def reference(base_weight, stacked_down_matrices, stacked_up_matrices, ranks, samples):
    coefficient = slot_scale(ranks, samples)
    block_rows = FF // N_ROW

    def merge_block(block_index):
        first_row = block_index * block_rows
        up_block = lax.dynamic_slice_in_dim(stacked_up_matrices, first_row, block_rows, 0)
        base_block = lax.dynamic_slice_in_dim(base_weight, first_row, block_rows, 0)
        scaled = (up_block.astype(jnp.float32) * coefficient[None, :]).astype(jnp.bfloat16)
        update = jnp.dot(scaled, stacked_down_matrices, preferred_element_type=jnp.float32)
        return (base_block.astype(jnp.float32) + update).astype(jnp.bfloat16)
    blocks = lax.map(merge_block, jnp.arange(N_ROW, dtype=jnp.int32))
    return blocks.reshape(FF, D)
```

```python
import functools

import jax
import jax.numpy as jnp
from jax import lax
from jax.experimental import pallas as pl
from jax.experimental.pallas import tpu as pltpu
from jax.sharding import PartitionSpec as P

RMAX = 64
ALPHA = 8.0
WIDTHS = (640, 768)
CHUNK = 512
VMEM_LIMIT = 16 * 2**20


def slot_scale(ranks, samples):
    counts = samples.astype(jnp.float32)
    fraction = counts / jnp.sum(counts)
    scale = fraction * ALPHA / jnp.sqrt(ranks.astype(jnp.float32))
    is_live = jnp.arange(RMAX, dtype=jnp.int32)[None, :] < ranks[:, None]
    return jnp.where(is_live, scale[:, None], jnp.float32(0.0)).reshape(-1)


def one_hot(ranks, group, clients, width):
    slots = clients * RMAX
    slot = lax.broadcasted_iota(jnp.int32, (1, slots), 1)
    client, m = slot // RMAX, slot % RMAX
    place = jnp.full((1, slots), -1, jnp.int32)
    start = jnp.int32(0)
    for k in range(clients):
        rank = ranks[group * clients + k]
        place = jnp.where((client == k) & (m < rank), start + m, place)
        start = start + rank
    row = lax.broadcasted_iota(jnp.int32, (width, slots), 0)
    return jnp.where(row == place, jnp.float32(1.0), jnp.float32(0.0)).astype(jnp.bfloat16)


def pack(up, ranks, group, width):
    rows, slots = up.shape
    half = rows // 2
    clients = slots // RMAX

    def kernel(ranks_ref, group_ref, up_ref, top_ref, bottom_ref):
        hot = one_hot(ranks_ref, group_ref[0], clients, width)
        for out_ref, at in ((top_ref, 0), (bottom_ref, half)):
            out_ref[...] = lax.dot_general(
                up_ref[at : at + half], hot, (((1,), (1,)), ((), ())), preferred_element_type=jnp.float32
            ).astype(jnp.bfloat16)

    return pl.pallas_call(
        kernel,
        grid_spec=pltpu.PrefetchScalarGridSpec(
            num_scalar_prefetch=2,
            grid=(1,),
            in_specs=[pl.BlockSpec((rows, slots), lambda i, *_: (0, 0))],
            out_specs=[pl.BlockSpec((half, width), lambda i, *_: (0, 0))] * 2,
        ),
        out_shape=[jax.ShapeDtypeStruct((half, width), jnp.bfloat16)] * 2,
        compiler_params=pltpu.CompilerParams(vmem_limit_bytes=VMEM_LIMIT),
        cost_estimate=pl.CostEstimate(flops=2 * rows * slots * width, bytes_accessed=4 * rows * slots, transcendentals=0),
        name="pack",
    )(ranks, group, up)


def unpack(ups, top, bottom, ranks, scale, group, packed):
    half, width = top.shape
    groups, _, slots = scale.shape
    clients = slots // RMAX

    def kernel(ranks_ref, group_ref, top_ref, bottom_ref, scale_ref, *rest):
        out_ref = rest[-1]
        if packed:
            hot = one_hot(ranks_ref, group_ref[0], clients, width)
        for in_ref, at in ((top_ref, 0), (bottom_ref, half)):
            if packed:
                whole = jnp.dot(in_ref[...], hot, preferred_element_type=jnp.float32)
            else:
                whole = in_ref[...].astype(jnp.float32)
            out_ref[0, at : at + half] = (whole * scale_ref[0]).astype(jnp.bfloat16)

    extra = [] if ups is None else [ups]
    return pl.pallas_call(
        kernel,
        grid_spec=pltpu.PrefetchScalarGridSpec(
            num_scalar_prefetch=2,
            grid=(1,),
            in_specs=[pl.BlockSpec((half, width), lambda i, *_: (0, 0))] * 2
            + [pl.BlockSpec((1, 1, slots), lambda i, ranks, group: (group[0], 0, 0))]
            + [pl.BlockSpec(memory_space=pl.ANY)] * len(extra),
            out_specs=pl.BlockSpec((1, 2 * half, slots), lambda i, ranks, group: (group[0], 0, 0)),
        ),
        out_shape=jax.ShapeDtypeStruct((groups, 2 * half, slots), jnp.bfloat16),
        input_output_aliases={5: 0} if extra else {},
        compiler_params=pltpu.CompilerParams(vmem_limit_bytes=VMEM_LIMIT),
        cost_estimate=pl.CostEstimate(flops=4 * half * slots * width, bytes_accessed=8 * half * slots, transcendentals=0),
        name="unpack",
    )(ranks, group, top, bottom, scale, *extra)


def pick(mine, other, core):
    rows, columns = mine.shape

    def kernel(core_ref, mine_ref, other_ref, out_ref):
        core = core_ref[0]
        out_ref[pl.ds(pl.multiple_of(core * rows, rows), rows)] = mine_ref[...]
        out_ref[pl.ds(pl.multiple_of((1 - core) * rows, rows), rows)] = other_ref[...]

    return pl.pallas_call(
        kernel,
        grid_spec=pltpu.PrefetchScalarGridSpec(
            num_scalar_prefetch=1,
            grid=(1,),
            in_specs=[pl.BlockSpec((rows, columns // 2), lambda i, core: (0, core[0]))] * 2,
            out_specs=pl.BlockSpec((2 * rows, columns // 2), lambda i, core: (0, 0)),
        ),
        out_shape=jax.ShapeDtypeStruct((2 * rows, columns // 2), mine.dtype),
        compiler_params=pltpu.CompilerParams(vmem_limit_bytes=VMEM_LIMIT),
        cost_estimate=pl.CostEstimate(flops=0, bytes_accessed=4 * rows * columns, transcendentals=0),
        name="pick",
    )(core, mine, other)


def merge(ups, lines, base, meta, block):
    _, rows, slots = ups.shape
    part = rows // 4
    piece = lines[0].shape[0] // 2
    tile = 256

    def kernel(meta_ref, block_ref, ups_ref, *refs):
        line_refs, base_ref, outs, total = refs[:8], refs[8], refs[9:13], refs[13]
        core = block_ref[2]
        at = block_ref[1]

        def columns(i, j):
            p, l = meta_ref[8 * core + 4 + j], meta_ref[8 * core + i]
            group = jnp.where(core == 0, p, l)
            inner = jnp.where(core == 0, l, p)
            return ups_ref[group, :, pl.ds(pl.multiple_of(inner * piece, piece), piece)]

        for i in range(4):
            left = jnp.concatenate([columns(i, j) for j in range(4)], axis=1)
            for n in range(CHUNK // tile):
                cols = pl.ds(pl.multiple_of(at * CHUNK + n * tile, tile), tile)
                right = jnp.concatenate([line_refs[2 * i][:, cols], line_refs[2 * i + 1][:, cols]], axis=0)
                product = jnp.dot(left, right, preferred_element_type=jnp.float32)
                if i == 0:
                    total[:, n * tile : (n + 1) * tile] = product
                else:
                    total[:, n * tile : (n + 1) * tile] += product
        for i, out in enumerate(outs):
            r = pl.ds(pl.multiple_of(meta_ref[16 + i] * part, 32), part)
            out[...] = (base_ref[r, :].astype(jnp.float32) + total[r, :]).astype(jnp.bfloat16)

    whole = pl.BlockSpec(memory_space=pltpu.VMEM)
    return pl.pallas_call(
        kernel,
        grid_spec=pltpu.PrefetchScalarGridSpec(
            num_scalar_prefetch=2,
            grid=(1,),
            in_specs=[whole] * 9 + [pl.BlockSpec((rows, CHUNK), lambda i, meta, block: (0, block[0]))],
            out_specs=[pl.BlockSpec((part, CHUNK), lambda i, *_: (0, 0))] * 4,
            scratch_shapes=[pltpu.VMEM((rows, CHUNK), jnp.float32)],
        ),
        out_shape=[jax.ShapeDtypeStruct((part, CHUNK), jnp.bfloat16)] * 4,
        compiler_params=pltpu.CompilerParams(vmem_limit_bytes=VMEM_LIMIT),
        cost_estimate=pl.CostEstimate(
            flops=2 * rows * 4 * slots * CHUNK, bytes_accessed=4 * rows * CHUNK, transcendentals=0
        ),
        name="merge",
    )(meta, block, pltpu.with_memory_space_constraint(ups, pltpu.VMEM),
      *[pltpu.with_memory_space_constraint(a, pltpu.VMEM) for a in lines], base)


def place(out, pieces, where, features):
    part, width = pieces[0].shape

    def kernel(where_ref, *refs):
        for i in range(4):

            @pl.when(pl.program_id(0) == i)
            def _(i=i):
                refs[-1][...] = refs[i][...]

    extra = [] if out is None else [out]
    return pl.pallas_call(
        kernel,
        grid_spec=pltpu.PrefetchScalarGridSpec(
            num_scalar_prefetch=1,
            grid=(4,),
            in_specs=[pl.BlockSpec((part, width), lambda i, where: (0, 0))] * 4
            + [pl.BlockSpec(memory_space=pl.ANY)] * len(extra),
            out_specs=pl.BlockSpec((part, width), lambda i, where: (0, where[i])),
        ),
        out_shape=jax.ShapeDtypeStruct((part, features), jnp.bfloat16),
        input_output_aliases={5: 0} if extra else {},
        compiler_params=pltpu.CompilerParams(vmem_limit_bytes=VMEM_LIMIT),
        cost_estimate=pl.CostEstimate(flops=0, bytes_accessed=16 * part * width, transcendentals=0),
        name="place",
    )(where, *pieces, *extra)


def ring(step):
    return [(i, (i + step) % 4) for i in range(4)]


def torus(step, first):
    pairs = []
    for x in range(4):
        for z in range(4):
            for core in range(2):
                along_x = (core == 0) == first
                to = ((x + step) % 4, z) if along_x else (x, (z + step) % 4)
                pairs.append(((x * 4 + z) * 2 + core, (to[0] * 4 + to[1]) * 2 + core))
    return pairs


SWAP = [(i, i ^ 1) for i in range(32)]


def program(width, base, down, up, ranks, samples):
    rows, slots = up.shape
    features = base.shape[1]
    packed = width < slots
    col = lax.axis_index("col").astype(jnp.int32)
    row = lax.axis_index("row").astype(jnp.int32)
    core, x, z = row % 2, row // 8, row // 2 % 4
    around = jnp.array([0, 3, 1, 2], jnp.int32)
    order = (col + around) % 4
    meta = jnp.concatenate([(z + around) % 4, (x + around) % 4, (x + around) % 4, (z + around) % 4, order])

    if packed:
        top, bottom = pack(up, ranks, order[:1], width)
    else:
        top, bottom = up[: rows // 2], up[rows // 2 :]
    left_top = lax.ppermute(top, "col", ring(1))
    right_bottom = lax.ppermute(bottom, "col", ring(3))
    left_bottom = lax.ppermute(bottom, "col", ring(1))
    right_top = lax.ppermute(top, "col", ring(3))
    far_top = lax.ppermute(left_top, "col", ring(1))
    far_bottom = lax.ppermute(right_bottom, "col", ring(3))

    mine = pick(down, lax.ppermute(down, "row", SWAP), core[None])
    piece_left = lax.ppermute(mine, "row", torus(1, True))
    piece_right = lax.ppermute(mine, "row", torus(3, True))
    piece_far = lax.ppermute(mine, "row", torus(2, True))
    line = [jnp.concatenate([mine, piece_left], axis=0), jnp.concatenate([piece_right, piece_far], axis=0)]
    line_left = [lax.ppermute(a, "row", torus(1, False)) for a in line]
    line_right = [lax.ppermute(a, "row", torus(3, False)) for a in line]
    line_far = [
        lax.ppermute(line_left[0], "row", torus(1, False)),
        lax.ppermute(line_right[1], "row", torus(3, False)),
    ]
    lines = line + line_left + line_right + line_far
    other_lines = [lax.ppermute(a, "row", SWAP) for a in lines]

    scale = slot_scale(ranks, samples).reshape(4, 1, slots)
    ups = unpack(None, up[: rows // 2], up[rows // 2 :], ranks, scale, order[:1], False)
    ups = unpack(ups, left_top, left_bottom, ranks, scale, order[1:2], packed)
    ups = unpack(ups, right_top, right_bottom, ranks, scale, order[2:3], packed)
    ups = unpack(ups, far_top, far_bottom, ranks, scale, order[3:4], packed)

    out = None
    blocks = features // 2 // CHUNK
    for half, from_lines in ((core, lines), (1 - core, other_lines)):
        for n in range(blocks):
            block = jnp.stack([half * blocks + n, jnp.int32(n), half])
            own, to_left, to_right, to_far = merge(ups, from_lines, base, meta, block)
            from_far = lax.ppermute(to_far, "col", ring(2))
            from_left = lax.ppermute(to_right, "col", ring(1))
            from_right = lax.ppermute(to_left, "col", ring(3))
            out = place(out, [own, from_left, from_right, from_far], order * (2 * blocks) + block[0], 4 * features)
    return out


def shards(base_weight, stacked_down_matrices, stacked_up_matrices, ranks, samples):
    slots = stacked_up_matrices.shape[1]
    most = jnp.max(jnp.sum(ranks.reshape(4, -1), axis=1))
    which = sum((most > width).astype(jnp.int32) for width in WIDTHS)
    return lax.switch(
        which,
        [functools.partial(program, width) for width in WIDTHS + (slots,)],
        base_weight,
        stacked_down_matrices,
        stacked_up_matrices,
        ranks,
        samples,
    )


def solution(mesh):
    placed = (P("row", "col"), P("row", "col"), P("row", "col"), P(), P())
    return jax.shard_map(
        shards, mesh=mesh, in_specs=placed, out_specs=P(("row", "col"), None), check_vma=False
    )
```

```python
import jax
import jax.numpy as jnp
from jax import lax
from jax.experimental import pallas as pl
from jax.experimental.pallas import tpu as pltpu
from jax.sharding import PartitionSpec as P

RMAX = 64
ALPHA = 8.0
WIDTH = 768
CHUNKS = (((0, 512), (512, 512)), ((0, 512), (512, 512)))
VMEM_LIMIT = 12 * 2**20
EARLY = 224
UNPACK_FLOPS = 30 * 10**9
MERGE_LIMIT = 22 * 2**20


def slot_scale(ranks, samples):
    counts = samples.astype(jnp.float32)
    fraction = counts / jnp.sum(counts)
    scale = fraction * ALPHA / jnp.sqrt(ranks.astype(jnp.float32))
    is_live = jnp.arange(RMAX, dtype=jnp.int32)[None, :] < ranks[:, None]
    return jnp.where(is_live, scale[:, None], jnp.float32(0.0)).reshape(-1)


def torus_place():
    row = lax.axis_index("row")
    return row // 8, (row // 2) % 4, row % 2


def near(at, i):
    return (at + (0, 3, 1, 2)[i]) % 4


def one_hot(ranks, group, slots, first, width):
    clients = slots // RMAX
    slot = lax.broadcasted_iota(jnp.int32, (1, slots), 1)
    client, m = slot // RMAX, slot % RMAX
    place = jnp.full((1, slots), -1, jnp.int32)
    start = jnp.int32(-first)
    for k in range(clients):
        rank = ranks[group * clients + k]
        place = jnp.where((client == k) & (m < rank), start + m, place)
        start = start + rank
    row = lax.broadcasted_iota(jnp.int32, (width, slots), 0)
    return jnp.where(row == place, jnp.float32(1.0), jnp.float32(0.0)).astype(jnp.bfloat16)


def pack(up, ranks, first, width):
    rows, slots = up.shape
    half = rows // 2
    clients = slots // RMAX

    def kernel(ranks_ref, up_ref, top_ref, bottom_ref, up_v, hot, sem):
        copies = []
        for j in range(2):
            span = pl.ds(j * half, half)
            copies.append(pltpu.make_async_copy(up_ref.at[span], up_v.at[span], sem.at[j]))
            copies[-1].start()
        group = lax.axis_index("col")
        m = lax.broadcasted_iota(jnp.int32, (RMAX, width), 0)
        ahead = lax.broadcasted_iota(jnp.int32, (RMAX, width), 1) - m
        start = jnp.int32(-first)
        for k in range(clients):
            rank = ranks_ref[group * clients + k]
            here = (ahead == start) & (m < rank)
            hot[k * RMAX : (k + 1) * RMAX] = jnp.where(here, jnp.float32(1.0), jnp.float32(0.0)).astype(jnp.bfloat16)
            start = start + rank
        for j, out_ref in enumerate((top_ref, bottom_ref)):
            copies[j].wait()
            out_ref[...] = jnp.dot(
                up_v[j * half : (j + 1) * half], hot[...], preferred_element_type=jnp.float32
            ).astype(jnp.bfloat16)

    return pl.pallas_call(
        kernel,
        grid_spec=pltpu.PrefetchScalarGridSpec(
            num_scalar_prefetch=1,
            grid=(1,),
            in_specs=[pl.BlockSpec(memory_space=pl.ANY)],
            out_specs=[pl.BlockSpec((half, width), lambda i, *_: (0, 0))] * 2,
            scratch_shapes=[
                pltpu.VMEM((rows, slots), jnp.bfloat16),
                pltpu.VMEM((slots, width), jnp.bfloat16),
                pltpu.SemaphoreType.DMA((2,)),
            ],
        ),
        out_shape=[jax.ShapeDtypeStruct((half, width), jnp.bfloat16)] * 2,
        compiler_params=pltpu.CompilerParams(vmem_limit_bytes=VMEM_LIMIT),
        cost_estimate=pl.CostEstimate(flops=2 * rows * slots * width, bytes_accessed=4 * rows * slots, transcendentals=0),
        name="pack",
    )(ranks, up)


def unpack(ups, items, rest, most, ranks, scale):
    groups, _, slots = scale.shape
    inner = slots // groups
    arrays = []
    for item in items:
        if not any(item[0] is a for a in arrays):
            arrays.append(item[0])
    index = [next(j for j, a in enumerate(arrays) if a is item[0]) for item in items]
    rows = items[0][0].shape[0] if ups is None else ups.shape[1]
    spill = slots - WIDTH
    n = len(arrays)

    def kernel(ranks_ref, most_ref, *refs):
        part_refs, scale_ref, rest_ref = refs[:n], refs[n], refs[n + 1]
        out_ref, rest_v, sem = refs[-3:]

        def put(group, at, value, add):
            for z in range(groups):
                cols = slice(z * inner, (z + 1) * inner)
                target = pl.ds(pl.multiple_of(group * inner, inner), inner)
                piece = value[:, cols]
                span = slice(at, at + value.shape[0])
                if add:
                    piece = piece + out_ref[group, span, cols]
                out_ref[group, span, cols] = piece
                out_ref[groups + z, span, target] = piece

        for which in range(groups):
            mine = [(j, item) for j, item in zip(index, items) if item[2] == which]
            if not mine:
                continue
            group = near(lax.axis_index("col"), which)
            factor = scale_ref[group]
            if which > 0:
                hot = one_hot(ranks_ref, group, slots, 0, WIDTH)
            for j, (_, first, _, at, count) in mine:
                part = part_refs[j][first : first + count]
                if which > 0:
                    whole = jnp.dot(part, hot, preferred_element_type=jnp.float32)
                else:
                    whole = part.astype(jnp.float32)
                put(group, at, (whole * factor).astype(jnp.bfloat16), False)
            if which > 0:

                @pl.when(most_ref[0] > WIDTH)
                def _(mine=mine, which=which, group=group, factor=factor):
                    copy = pltpu.make_async_copy(rest_ref.at[:, (which - 1) * spill : which * spill], rest_v, sem)
                    copy.start()
                    copy.wait()
                    hot = one_hot(ranks_ref, group, slots, WIDTH, spill)
                    for _, (_, _, _, at, count) in mine:
                        whole = jnp.dot(rest_v[at : at + count], hot, preferred_element_type=jnp.float32)
                        put(group, at, (whole * factor).astype(jnp.bfloat16), True)

    whole = pl.BlockSpec(memory_space=pltpu.VMEM)
    vmem = lambda a: pltpu.with_memory_space_constraint(a, pltpu.VMEM)
    extra = [] if ups is None else [vmem(ups)]
    return pl.pallas_call(
        kernel,
        grid_spec=pltpu.PrefetchScalarGridSpec(
            num_scalar_prefetch=2,
            grid=(1,),
            in_specs=[whole] * (n + 1) + [pl.BlockSpec(memory_space=pl.ANY)] + [whole] * len(extra),
            out_specs=whole,
            scratch_shapes=[pltpu.VMEM((rows, spill), jnp.bfloat16), pltpu.SemaphoreType.DMA],
        ),
        out_shape=pltpu.VMEM((2 * groups, rows, slots), jnp.bfloat16),
        input_output_aliases={n + 4: 0} if extra else {},
        compiler_params=pltpu.CompilerParams(vmem_limit_bytes=VMEM_LIMIT),
        cost_estimate=pl.CostEstimate(flops=UNPACK_FLOPS, bytes_accessed=6 * rows * slots, transcendentals=0),
        name="unpack",
    )(ranks, most, *[vmem(a) for a in arrays], scale, rest, *extra)


def pick(mine, other):
    rows, columns = mine.shape

    def kernel(mine_ref, other_ref, out_ref):
        core = lax.axis_index("row") % 2
        out_ref[pl.ds(pl.multiple_of(core * rows, rows), rows)] = mine_ref[...]
        out_ref[pl.ds(pl.multiple_of((1 - core) * rows, rows), rows)] = other_ref[...]

    return pl.pallas_call(
        kernel,
        grid=(1,),
        in_specs=[pl.BlockSpec((rows, columns // 2), lambda i: (0, lax.axis_index("row") % 2))] * 2,
        out_specs=pl.BlockSpec((2 * rows, columns // 2), lambda i: (0, 0)),
        out_shape=jax.ShapeDtypeStruct((2 * rows, columns // 2), mine.dtype),
        compiler_params=pltpu.CompilerParams(vmem_limit_bytes=VMEM_LIMIT),
        cost_estimate=pl.CostEstimate(flops=0, bytes_accessed=4 * rows * columns, transcendentals=0),
        name="pick",
    )(mine, other)


def halves(upper_of, lower_of):
    rows, columns = upper_of.shape
    half = rows // 2

    def kernel(a_ref, b_ref, upper_ref, lower_ref, sem):
        copies = [
            pltpu.make_async_copy(a_ref.at[pl.ds(0, half)], upper_ref, sem.at[0]),
            pltpu.make_async_copy(b_ref.at[pl.ds(half, half)], lower_ref, sem.at[1]),
        ]
        for copy in copies:
            copy.start()
        for copy in copies:
            copy.wait()

    return pl.pallas_call(
        kernel,
        in_specs=[pl.BlockSpec(memory_space=pl.ANY)] * 2,
        out_specs=[pl.BlockSpec(memory_space=pl.ANY)] * 2,
        out_shape=[jax.ShapeDtypeStruct((half, columns), upper_of.dtype)] * 2,
        scratch_shapes=[pltpu.SemaphoreType.DMA((2,))],
        compiler_params=pltpu.CompilerParams(vmem_limit_bytes=VMEM_LIMIT),
        cost_estimate=pl.CostEstimate(flops=0, bytes_accessed=4 * rows * columns, transcendentals=0),
        name="halves",
    )(upper_of, lower_of)


def line_up(pieces):
    rows, columns = pieces[0].shape

    def kernel(*refs):
        x, z, core = torus_place()
        at = jnp.where(core == 0, x, z)
        for i in range(4):
            refs[4][pl.ds(pl.multiple_of(near(at, i) * rows, rows), rows)] = refs[i][...]

    return pl.pallas_call(
        kernel,
        out_shape=jax.ShapeDtypeStruct((4 * rows, columns), pieces[0].dtype),
        compiler_params=pltpu.CompilerParams(vmem_limit_bytes=VMEM_LIMIT),
        cost_estimate=pl.CostEstimate(flops=0, bytes_accessed=16 * rows * columns, transcendentals=0),
        name="line_up",
    )(*pieces)


def merge(ups, lines, base, theirs, at, width):
    _, rows, slots = ups.shape
    part = rows // 4
    features = base.shape[1]

    def half():
        core = lax.axis_index("row") % 2
        return 1 - core if theirs else core

    def kernel(ups_ref, l0, l1, l2, l3, l4, base_ref, o0, o1, o2, o3, d_v, base_v, total, d_sem, base_sem):
        x, z, _ = torus_place()
        core = half()
        along = jnp.where(core == 0, z, x)
        first = jnp.where(core == 0, 4, 0)
        where = ((l0, slots), (l1, slots), (l2, slots), (l3, slots // 2), (l4, slots // 2))
        copies = []
        row = 0
        for j, (line, count) in enumerate(where):
            copies.append(pltpu.make_async_copy(line.at[:, pl.ds(at, width)], d_v.at[pl.ds(row, count)], d_sem.at[j]))
            row += count
        base_at = pl.ds(pl.multiple_of(half() * (features // 2) + at, width), width)
        copies.append(pltpu.make_async_copy(base_ref.at[:, base_at], base_v, base_sem))
        for copy in copies:
            copy.start()
        for i in range(4):
            for copy in copies[i:] if i == 3 else copies[i : i + 1]:
                copy.wait()
            product = jnp.dot(
                ups_ref[first + near(along, i)], d_v[i * slots : (i + 1) * slots], preferred_element_type=jnp.float32
            )
            if i == 0:
                total[...] = product
            else:
                total[...] += product
        col = lax.axis_index("col")
        for i, out in enumerate((o0, o1, o2, o3)):
            r = pl.ds(pl.multiple_of(near(col, i) * part, 32), part)
            out[...] = (base_v[r, :].astype(jnp.float32) + total[r, :]).astype(jnp.bfloat16)

    hold = pl.BlockSpec(memory_space=pl.ANY)
    return pl.pallas_call(
        kernel,
        grid=(1,),
        in_specs=[pl.BlockSpec(memory_space=pltpu.VMEM)] + [hold] * 6,
        out_specs=[pl.BlockSpec((part, width), lambda i: (0, 0))] * 4,
        scratch_shapes=[
            pltpu.VMEM((4 * slots, width), jnp.bfloat16),
            pltpu.VMEM((rows, width), jnp.bfloat16),
            pltpu.VMEM((rows, width), jnp.float32),
            pltpu.SemaphoreType.DMA((5,)),
            pltpu.SemaphoreType.DMA,
        ],
        out_shape=[jax.ShapeDtypeStruct((part, width), jnp.bfloat16)] * 4,
        compiler_params=pltpu.CompilerParams(vmem_limit_bytes=MERGE_LIMIT),
        cost_estimate=pl.CostEstimate(flops=2 * rows * 4 * slots * width, bytes_accessed=4 * rows * width, transcendentals=0),
        name="merge",
    )(pltpu.with_memory_space_constraint(ups, pltpu.VMEM), *lines, base)


def place(pieces, features):
    part = pieces[0][0].shape[0]
    count = len(pieces[0])
    flat = [a for row in pieces for a in row]
    starts = [(theirs, at, width) for theirs in (False, True) for at, width in CHUNKS[theirs]]

    def kernel(*refs):
        core = lax.axis_index("row") % 2
        n = pl.program_id(0)
        for i in range(4):

            @pl.when(near(lax.axis_index("col"), i) == n)
            def _(i=i):
                for j, (theirs, at, width) in enumerate(starts):
                    half = 1 - core if theirs else core
                    cols = pl.ds(pl.multiple_of(half * (features // 8) + at, 128), width)
                    refs[-1][:, cols] = refs[i * count + j][...]

    return pl.pallas_call(
        kernel,
        grid=(4,),
        in_specs=[pl.BlockSpec(a.shape, lambda n: (0, 0)) for a in flat],
        out_specs=pl.BlockSpec((part, features // 4), lambda n: (0, n)),
        out_shape=jax.ShapeDtypeStruct((part, features), jnp.bfloat16),
        compiler_params=pltpu.CompilerParams(vmem_limit_bytes=VMEM_LIMIT),
        cost_estimate=pl.CostEstimate(flops=0, bytes_accessed=4 * part * features, transcendentals=0),
        name="place",
    )(*flat)


def ring(step):
    return [(i, (i + step) % 4) for i in range(4)]


def torus(step, first):
    pairs = []
    for x in range(4):
        for z in range(4):
            for core in range(2):
                along_x = (core == 0) == first
                to = ((x + step) % 4, z) if along_x else (x, (z + step) % 4)
                pairs.append(((x * 4 + z) * 2 + core, (to[0] * 4 + to[1]) * 2 + core))
    return pairs


SWAP = [(i, i ^ 1) for i in range(32)]


def after(value, *others):
    return lax.optimization_barrier((value, *others))[0]


def shards(base, down, up, ranks, samples):
    rows, slots = up.shape
    features = base.shape[1]

    half = rows // 2
    top, bottom = pack(up, ranks, 0, WIDTH)
    mine = pick(down, lax.ppermute(down, "row", SWAP))
    mine, top, bottom = lax.optimization_barrier((mine, top, bottom))

    left_top = lax.ppermute(top, "col", ring(1))
    right_bottom = lax.ppermute(bottom, "col", ring(3))
    piece_far = lax.ppermute(mine, "row", torus(2, True))
    piece_left = lax.ppermute(mine, "row", torus(1, True))
    piece_right = lax.ppermute(mine, "row", torus(3, True))

    most = jnp.max(jnp.sum(ranks.reshape(4, -1), axis=1))

    def send_rest(up, ranks):
        own = jnp.concatenate(pack(up, ranks, WIDTH, slots - WIDTH))
        return jnp.concatenate([lax.ppermute(own, "col", ring(k)) for k in (1, 3, 2)], axis=1)

    def no_rest(up, ranks):
        return jnp.zeros((rows, 3 * (slots - WIDTH)), jnp.bfloat16)

    rest = lax.cond(most > WIDTH, send_rest, no_rest, up, ranks)
    most = most.reshape(1)
    scale = slot_scale(ranks, samples).reshape(4, 1, slots)
    ups = unpack(None, [(up, 0, 0, 0, rows)], rest, most, ranks, scale)
    mine, piece_left, piece_right, piece_far, left_top, right_bottom, top, bottom, ups = lax.optimization_barrier(
        (mine, piece_left, piece_right, piece_far, left_top, right_bottom, top, bottom, ups)
    )

    line = line_up([mine, piece_left, piece_right, piece_far])
    line_left = lax.ppermute(line, "row", torus(1, False))
    line_right = lax.ppermute(line, "row", torus(3, False))
    from_left = lax.ppermute(jnp.concatenate([bottom, left_top[:EARLY]]), "col", ring(1))
    from_right = lax.ppermute(jnp.concatenate([top, right_bottom[:EARLY]]), "col", ring(3))
    line_there = lax.ppermute(line, "row", SWAP)
    ups = unpack(ups, [(left_top, 0, 1, 0, half), (right_bottom, 0, 2, half, half)], rest, most, ranks, scale)
    line, line_left, line_right, from_left, from_right, line_there, left_top, right_bottom, ups = (
        lax.optimization_barrier(
            (line, line_left, line_right, from_left, from_right, line_there, left_top, right_bottom, ups)
        )
    )

    upper, lower = halves(line_left, line_right)
    line_far = [lax.ppermute(upper, "row", torus(1, False)), lax.ppermute(lower, "row", torus(3, False))]
    late_left = lax.ppermute(left_top[EARLY:], "col", ring(1))
    late_right = lax.ppermute(right_bottom[EARLY:], "col", ring(3))
    left_there = lax.ppermute(line_left, "row", SWAP)
    ups = unpack(
        ups,
        [
            (from_left, 0, 1, half, half),
            (from_right, 0, 2, 0, half),
            (from_left, half, 3, 0, EARLY),
            (from_right, half, 3, half, EARLY),
        ],
        rest, most, ranks, scale,
    )
    *line_far, late_left, late_right, left_there, ups = lax.optimization_barrier(
        (*line_far, late_left, late_right, left_there, ups)
    )
    ups = unpack(
        ups,
        [(late_left, 0, 3, EARLY, half - EARLY), (late_right, 0, 3, half + EARLY, half - EARLY)],
        rest, most, ranks, scale,
    )
    lines = [line, line_left, line_right, *line_far]
    other_lines = [line_there, left_there] + [lax.ppermute(a, "row", SWAP) for a in lines[2:]]

    pieces = [[], [], [], []]
    for theirs, from_lines in ((False, lines), (True, other_lines)):
        for at, width in CHUNKS[theirs]:
            if len(pieces[0]) == 1:
                ups, *other_lines[2:] = lax.optimization_barrier((ups, *other_lines[2:]))
            own, to_left, to_right, to_far = merge(ups, from_lines, base, theirs, at, width)
            from_far = lax.ppermute(to_far, "col", ring(2))
            from_left = lax.ppermute(to_right, "col", ring(1))
            from_right = lax.ppermute(to_left, "col", ring(3))
            for row, piece in zip(pieces, (own, from_left, from_right, from_far)):
                row.append(piece)
    return place(pieces, 4 * features)


def solution(mesh):
    placed = (P("row", "col"), P("row", "col"), P("row", "col"), P(), P())
    return jax.shard_map(
        shards, mesh=mesh, in_specs=placed, out_specs=P(("row", "col"), None), check_vma=False
    )
```

```python
import jax
import jax.numpy as jnp
from jax import lax
from jax.experimental import pallas as pl
from jax.experimental.pallas import tpu as pltpu
from jax.sharding import PartitionSpec as P

RMAX = 64
ALPHA = 8.0
WIDTH = 768
CHUNK = 512
CHUNKS = (((0, 512), (512, 512)), ((0, 512), (512, 512)))
VMEM_LIMIT = 12 * 2**20
EARLY = 160
UNPACK_FLOPS = 30 * 10**9
MERGE_LIMIT = 22 * 2**20


def torus_place():
    row = lax.axis_index("row")
    return row // 8, (row // 2) % 4, row % 2


def near(at, i):
    return (at + (0, 3, 1, 2)[i]) % 4


def slot_scale(ranks, samples, group, slots):
    clients = slots // RMAX
    total = jnp.int32(0)
    for k in range(samples.shape[0]):
        total = total + samples[k]
    slot = lax.broadcasted_iota(jnp.int32, (1, slots), 1)
    client, m = slot // RMAX, slot % RMAX
    rank = jnp.ones((1, slots), jnp.int32)
    count = jnp.ones((1, slots), jnp.int32)
    for k in range(clients):
        rank = jnp.where(client == k, ranks[group * clients + k], rank)
        count = jnp.where(client == k, samples[group * clients + k], count)
    fraction = count.astype(jnp.float32) / jnp.full((1, slots), total, jnp.int32).astype(jnp.float32)
    scale = fraction * ALPHA / jnp.sqrt(rank.astype(jnp.float32))
    return jnp.where(m < rank, scale, jnp.float32(0.0))


def one_hot(ranks, group, slots, first, width):
    clients = slots // RMAX
    slot = lax.broadcasted_iota(jnp.int32, (1, slots), 1)
    client, m = slot // RMAX, slot % RMAX
    place = jnp.full((1, slots), -1, jnp.int32)
    start = jnp.int32(0)
    for k in range(clients):
        rank = ranks[group * clients + k]
        place = jnp.where((client == k) & (m < rank), start + m, place)
        start = start + rank
    row = lax.broadcasted_iota(jnp.int32, (width, slots), 0) + first
    return jnp.where(row == place, jnp.float32(1.0), jnp.float32(0.0)).astype(jnp.bfloat16), start


def pack(up, ranks, first, width):
    rows, slots = up.shape
    half = rows // 2
    clients = slots // RMAX

    def kernel(ranks_ref, up_ref, top_ref, bottom_ref, up_v, hot, sem):
        copies = []
        for j in range(2):
            span = pl.ds(j * half, half)
            copies.append(pltpu.make_async_copy(up_ref.at[span], up_v.at[span], sem.at[j]))
            copies[-1].start()
        group = lax.axis_index("col")
        m = lax.broadcasted_iota(jnp.int32, (RMAX, width), 0)
        ahead = lax.broadcasted_iota(jnp.int32, (RMAX, width), 1) - m
        start = jnp.int32(-first)
        for k in range(clients):
            rank = ranks_ref[group * clients + k]
            here = (ahead == start) & (m < rank)
            hot[k * RMAX : (k + 1) * RMAX] = jnp.where(here, jnp.float32(1.0), jnp.float32(0.0)).astype(jnp.bfloat16)
            start = start + rank
        for j, out_ref in enumerate((top_ref, bottom_ref)):
            copies[j].wait()
            out_ref[...] = jnp.dot(
                up_v[j * half : (j + 1) * half], hot[...], preferred_element_type=jnp.float32
            ).astype(jnp.bfloat16)

    return pl.pallas_call(
        kernel,
        grid_spec=pltpu.PrefetchScalarGridSpec(
            num_scalar_prefetch=1,
            grid=(1,),
            in_specs=[pl.BlockSpec(memory_space=pl.ANY)],
            out_specs=[pl.BlockSpec((half, width), lambda i, *_: (0, 0))] * 2,
            scratch_shapes=[
                pltpu.VMEM((rows, slots), jnp.bfloat16),
                pltpu.VMEM((slots, width), jnp.bfloat16),
                pltpu.SemaphoreType.DMA((2,)),
            ],
        ),
        out_shape=[jax.ShapeDtypeStruct((half, width), jnp.bfloat16)] * 2,
        compiler_params=pltpu.CompilerParams(vmem_limit_bytes=VMEM_LIMIT),
        cost_estimate=pl.CostEstimate(flops=2 * rows * slots * width, bytes_accessed=4 * rows * slots, transcendentals=0),
        name="pack",
    )(ranks, up)


def unpack(ups, items, rest, ranks, samples, slots):
    groups = 4
    inner = slots // groups
    arrays = []
    for item in items:
        if not any(item[0] is a for a in arrays):
            arrays.append(item[0])
    index = [next(j for j, a in enumerate(arrays) if a is item[0]) for item in items]
    rows = items[0][0].shape[0] if ups is None else ups.shape[1]
    spill = slots - WIDTH
    n = len(arrays)

    def kernel(ranks_ref, samples_ref, *refs):
        part_refs, rest_ref = refs[:n], refs[n]
        out_ref, rest_v, sem = refs[-3:]

        def put(group, at, value, add):
            for z in range(groups):
                cols = slice(z * inner, (z + 1) * inner)
                target = pl.ds(pl.multiple_of(group * inner, inner), inner)
                piece = value[:, cols]
                span = slice(at, at + value.shape[0])
                if add:
                    piece = piece + out_ref[group, span, cols]
                out_ref[group, span, cols] = piece
                out_ref[groups + z, span, target] = piece

        for which in range(groups):
            mine = [(j, item) for j, item in zip(index, items) if item[2] == which]
            if not mine:
                continue
            group = near(lax.axis_index("col"), which)
            factor = slot_scale(ranks_ref, samples_ref, group, slots)
            if which > 0:
                hot, live = one_hot(ranks_ref, group, slots, 0, WIDTH)
            for j, (_, first, _, at, count) in mine:
                part = part_refs[j][first : first + count]
                if which > 0:
                    whole = jnp.dot(part, hot, preferred_element_type=jnp.float32)
                else:
                    whole = part.astype(jnp.float32)
                put(group, at, (whole * factor).astype(jnp.bfloat16), False)
            if which > 0:

                @pl.when(live > WIDTH)
                def _(mine=mine, which=which, group=group, factor=factor):
                    copy = pltpu.make_async_copy(rest_ref.at[:, (which - 1) * spill : which * spill], rest_v, sem)
                    copy.start()
                    copy.wait()
                    hot, _ = one_hot(ranks_ref, group, slots, WIDTH, spill)
                    for _, (_, _, _, at, count) in mine:
                        whole = jnp.dot(rest_v[at : at + count], hot, preferred_element_type=jnp.float32)
                        put(group, at, (whole * factor).astype(jnp.bfloat16), True)

    whole = pl.BlockSpec(memory_space=pltpu.VMEM)
    vmem = lambda a: pltpu.with_memory_space_constraint(a, pltpu.VMEM)
    extra = [] if ups is None else [vmem(ups)]
    return pl.pallas_call(
        kernel,
        grid_spec=pltpu.PrefetchScalarGridSpec(
            num_scalar_prefetch=2,
            grid=(1,),
            in_specs=[whole] * n + [pl.BlockSpec(memory_space=pl.ANY)] + [whole] * len(extra),
            out_specs=whole,
            scratch_shapes=[pltpu.VMEM((rows, spill), jnp.bfloat16), pltpu.SemaphoreType.DMA],
        ),
        out_shape=pltpu.VMEM((2 * groups, rows, slots), jnp.bfloat16),
        input_output_aliases={n + 3: 0} if extra else {},
        compiler_params=pltpu.CompilerParams(vmem_limit_bytes=VMEM_LIMIT),
        cost_estimate=pl.CostEstimate(flops=UNPACK_FLOPS, bytes_accessed=6 * rows * slots, transcendentals=0),
        name="unpack",
    )(ranks, samples, *[vmem(a) for a in arrays], rest, *extra)


def pick(mine, other):
    rows, columns = mine.shape

    def kernel(mine_ref, other_ref, out_ref):
        core = lax.axis_index("row") % 2
        for n in range(columns // 2 // CHUNK):
            cols = slice(n * CHUNK, (n + 1) * CHUNK)
            out_ref[n, pl.ds(pl.multiple_of(core * rows, rows), rows)] = mine_ref[:, cols]
            out_ref[n, pl.ds(pl.multiple_of((1 - core) * rows, rows), rows)] = other_ref[:, cols]

    return pl.pallas_call(
        kernel,
        grid=(1,),
        in_specs=[pl.BlockSpec((rows, columns // 2), lambda i: (0, lax.axis_index("row") % 2))] * 2,
        out_specs=pl.BlockSpec((columns // 2 // CHUNK, 2 * rows, CHUNK), lambda i: (0, 0, 0)),
        out_shape=jax.ShapeDtypeStruct((columns // 2 // CHUNK, 2 * rows, CHUNK), mine.dtype),
        compiler_params=pltpu.CompilerParams(vmem_limit_bytes=VMEM_LIMIT),
        cost_estimate=pl.CostEstimate(flops=0, bytes_accessed=4 * rows * columns, transcendentals=0),
        name="pick",
    )(mine, other)


def halves(upper_of, lower_of):
    chunks, rows, columns = upper_of.shape
    half = rows // 2

    def kernel(a_ref, b_ref, upper_ref, lower_ref, sem):
        copies = [
            pltpu.make_async_copy(a_ref.at[:, pl.ds(0, half)], upper_ref, sem.at[0]),
            pltpu.make_async_copy(b_ref.at[:, pl.ds(half, half)], lower_ref, sem.at[1]),
        ]
        for copy in copies:
            copy.start()
        for copy in copies:
            copy.wait()

    return pl.pallas_call(
        kernel,
        in_specs=[pl.BlockSpec(memory_space=pl.ANY)] * 2,
        out_specs=[pl.BlockSpec(memory_space=pl.ANY)] * 2,
        out_shape=[jax.ShapeDtypeStruct((chunks, half, columns), upper_of.dtype)] * 2,
        scratch_shapes=[pltpu.SemaphoreType.DMA((2,))],
        compiler_params=pltpu.CompilerParams(vmem_limit_bytes=VMEM_LIMIT),
        cost_estimate=pl.CostEstimate(flops=0, bytes_accessed=4 * rows * columns, transcendentals=0),
        name="halves",
    )(upper_of, lower_of)


def line_up(pieces):
    chunks, rows, columns = pieces[0].shape

    def kernel(*refs):
        x, z, core = torus_place()
        at = jnp.where(core == 0, x, z)
        for i in range(4):
            refs[4][:, pl.ds(pl.multiple_of(near(at, (3, 1, 2, 0)[i]) * rows, rows), rows)] = refs[i][...]

    return pl.pallas_call(
        kernel,
        out_shape=jax.ShapeDtypeStruct((chunks, 4 * rows, columns), pieces[0].dtype),
        compiler_params=pltpu.CompilerParams(vmem_limit_bytes=VMEM_LIMIT),
        cost_estimate=pl.CostEstimate(flops=0, bytes_accessed=16 * chunks * rows * columns, transcendentals=0),
        name="line_up",
    )(*pieces)


def merge(ups, lines, base, theirs, at, width):
    _, rows, slots = ups.shape
    part = rows // 4
    features = base.shape[1]

    def half():
        core = lax.axis_index("row") % 2
        return 1 - core if theirs else core

    def kernel(ups_ref, l0, l1, l2, l3, l4, base_ref, o0, o1, o2, o3, d_v, base_v, total, d_sem, base_sem):
        x, z, _ = torus_place()
        core = half()
        along = jnp.where(core == 0, z, x)
        first = jnp.where(core == 0, 4, 0)
        where = ((l0, slots), (l1, slots), (l2, slots), (l3, slots // 2), (l4, slots // 2))
        copies = []
        row = 0
        for j, (line, count) in enumerate(where):
            copies.append(pltpu.make_async_copy(line.at[at // width], d_v.at[pl.ds(row, count)], d_sem.at[j]))
            row += count
        base_at = pl.ds(pl.multiple_of(half() * (features // 2) + at, width), width)
        copies.append(pltpu.make_async_copy(base_ref.at[:, base_at], base_v, base_sem))
        for copy in copies:
            copy.start()
        for i in range(4):
            for copy in copies[i:] if i == 3 else copies[i : i + 1]:
                copy.wait()
            product = jnp.dot(
                ups_ref[first + near(along, i)], d_v[i * slots : (i + 1) * slots], preferred_element_type=jnp.float32
            )
            if i == 0:
                total[...] = product
            else:
                total[...] += product
        col = lax.axis_index("col")
        for i, out in enumerate((o0, o1, o2, o3)):
            r = pl.ds(pl.multiple_of(near(col, i) * part, 32), part)
            out[...] = (base_v[r, :].astype(jnp.float32) + total[r, :]).astype(jnp.bfloat16)

    hold = pl.BlockSpec(memory_space=pl.ANY)
    return pl.pallas_call(
        kernel,
        grid=(1,),
        in_specs=[pl.BlockSpec(memory_space=pltpu.VMEM)] + [hold] * 6,
        out_specs=[pl.BlockSpec((part, width), lambda i: (0, 0))] * 4,
        scratch_shapes=[
            pltpu.VMEM((4 * slots, width), jnp.bfloat16),
            pltpu.VMEM((rows, width), jnp.bfloat16),
            pltpu.VMEM((rows, width), jnp.float32),
            pltpu.SemaphoreType.DMA((5,)),
            pltpu.SemaphoreType.DMA,
        ],
        out_shape=[jax.ShapeDtypeStruct((part, width), jnp.bfloat16)] * 4,
        compiler_params=pltpu.CompilerParams(vmem_limit_bytes=MERGE_LIMIT),
        cost_estimate=pl.CostEstimate(flops=2 * rows * 4 * slots * width, bytes_accessed=4 * rows * width, transcendentals=0),
        name="merge",
    )(pltpu.with_memory_space_constraint(ups, pltpu.VMEM), *lines, base)


def place(out, pieces, chunk, features):
    part, width = pieces[0].shape
    theirs, at = chunk

    def block(n):
        core = lax.axis_index("row") % 2
        half = 1 - core if theirs else core
        return n * (features // 4 // width) + half * (features // 8 // width) + at // width

    def kernel(*refs):
        for i in range(4):

            @pl.when(near(lax.axis_index("col"), (3, 1, 2, 0)[i]) == pl.program_id(0))
            def _(i=i):
                refs[-1][...] = refs[i][...]

    extra = [] if out is None else [out]
    return pl.pallas_call(
        kernel,
        grid=(4,),
        in_specs=[pl.BlockSpec((part, width), lambda n: (0, 0))] * 4 + [pl.BlockSpec(memory_space=pl.ANY)] * len(extra),
        out_specs=pl.BlockSpec((part, width), lambda n: (0, block(n))),
        out_shape=jax.ShapeDtypeStruct((part, features), jnp.bfloat16),
        input_output_aliases={4: 0} if extra else {},
        compiler_params=pltpu.CompilerParams(vmem_limit_bytes=VMEM_LIMIT),
        cost_estimate=pl.CostEstimate(flops=0, bytes_accessed=16 * part * width, transcendentals=0),
        name="place",
    )(*pieces, *extra)


def ring(step):
    return [(i, (i + step) % 4) for i in range(4)]


def torus(step, first):
    pairs = []
    for x in range(4):
        for z in range(4):
            for core in range(2):
                along_x = (core == 0) == first
                to = ((x + step) % 4, z) if along_x else (x, (z + step) % 4)
                pairs.append(((x * 4 + z) * 2 + core, (to[0] * 4 + to[1]) * 2 + core))
    return pairs


SWAP = [(i, i ^ 1) for i in range(32)]


def after(value, *others):
    return lax.optimization_barrier((value, *others))[0]


def shards(base, down, up, ranks, samples):
    rows, slots = up.shape
    features = base.shape[1]

    half = rows // 2
    top, bottom = pack(up, ranks, 0, WIDTH)
    mine = pick(down, lax.ppermute(down, "row", SWAP))
    mine, top, bottom = lax.optimization_barrier((mine, top, bottom))

    left_top = lax.ppermute(top, "col", ring(1))
    right_bottom = lax.ppermute(bottom, "col", ring(3))
    def send_rest(up, ranks):
        own = jnp.concatenate(pack(up, ranks, WIDTH, slots - WIDTH))
        return jnp.concatenate([lax.ppermute(own, "col", ring(k)) for k in (1, 3, 2)], axis=1)

    def no_rest(up, ranks):
        return jnp.zeros((rows, 3 * (slots - WIDTH)), jnp.bfloat16)

    most = jnp.max(jnp.sum(ranks.reshape(4, -1), axis=1))
    rest = lax.cond(most > WIDTH, send_rest, no_rest, up, ranks)
    ups = unpack(None, [(up, 0, 0, 0, rows)], rest, ranks, samples, slots)
    mine, ups = lax.optimization_barrier((mine, ups))
    piece_far = lax.ppermute(mine, "row", torus(2, True))
    piece_left = lax.ppermute(mine, "row", torus(1, True))
    piece_right = lax.ppermute(mine, "row", torus(3, True))
    piece_far, piece_left, piece_right, mine, left_top, right_bottom, top, bottom, ups = lax.optimization_barrier(
        (piece_far, piece_left, piece_right, mine, left_top, right_bottom, top, bottom, ups)
    )

    line = line_up([piece_far, piece_left, piece_right, mine])
    line_left = lax.ppermute(line, "row", torus(1, False))
    line_right = lax.ppermute(line, "row", torus(3, False))
    from_left = lax.ppermute(jnp.concatenate([bottom, left_top[:EARLY]]), "col", ring(1))
    from_right = lax.ppermute(jnp.concatenate([top, right_bottom[:EARLY]]), "col", ring(3))
    line_there = lax.ppermute(line, "row", SWAP)
    ups = unpack(ups, [(left_top, 0, 1, 0, half), (right_bottom, 0, 2, half, half)], rest, ranks, samples, slots)
    line, line_left, line_right, from_left, from_right, line_there, left_top, right_bottom, ups = (
        lax.optimization_barrier(
            (line, line_left, line_right, from_left, from_right, line_there, left_top, right_bottom, ups)
        )
    )

    upper, lower = halves(line_left, line_right)
    line_far = [lax.ppermute(upper, "row", torus(1, False)), lax.ppermute(lower, "row", torus(3, False))]
    late_left = lax.ppermute(left_top[EARLY:], "col", ring(1))
    late_right = lax.ppermute(right_bottom[EARLY:], "col", ring(3))
    left_there = lax.ppermute(line_left, "row", SWAP)
    ups = unpack(
        ups,
        [
            (from_left, 0, 1, half, half),
            (from_right, 0, 2, 0, half),
            (from_left, half, 3, 0, EARLY),
            (from_right, half, 3, half, EARLY),
        ],
        rest, ranks, samples, slots,
    )
    *line_far, late_left, late_right, left_there, ups = lax.optimization_barrier(
        (*line_far, late_left, late_right, left_there, ups)
    )
    ups = unpack(
        ups,
        [(late_left, 0, 3, EARLY, half - EARLY), (late_right, 0, 3, half + EARLY, half - EARLY)],
        rest, ranks, samples, slots,
    )
    lines = [line, line_left, line_right, *line_far]
    other_lines = [line_there, left_there] + [lax.ppermute(a, "row", SWAP) for a in lines[2:]]

    out, first = None, True
    for theirs, from_lines in ((False, lines), (True, other_lines)):
        for at, width in CHUNKS[theirs]:
            if not first and not theirs:
                ups, *other_lines[2:] = lax.optimization_barrier((ups, *other_lines[2:]))
            first = False
            own, to_left, to_right, to_far = merge(ups, from_lines, base, theirs, at, width)
            from_far = lax.ppermute(to_far, "col", ring(2))
            from_left = lax.ppermute(to_right, "col", ring(1))
            from_right = lax.ppermute(to_left, "col", ring(3))
            out = place(out, [from_far, from_left, from_right, own], (theirs, at), 4 * features)
    return out


def solution(mesh):
    placed = (P("row", "col"), P("row", "col"), P("row", "col"), P(), P())
    return jax.shard_map(
        shards, mesh=mesh, in_specs=placed, out_specs=P(("row", "col"), None), check_vma=False
    )
```

```python
import jax
import jax.numpy as jnp
from jax import lax
from jax.experimental import pallas as pl
from jax.experimental.pallas import tpu as pltpu
from jax.sharding import PartitionSpec as P

RMAX = 64
ALPHA = 8.0
WIDTH = 768
CHUNK = 512
CHUNKS = (((0, 512), (512, 512)), ((0, 512), (512, 512)))
VMEM_LIMIT = 12 * 2**20
EARLY = 176
UNPACK_FLOPS = 30 * 10**9
MERGE_LIMIT = 22 * 2**20


def torus_place():
    row = lax.axis_index("row")
    return row // 8, (row // 2) % 4, row % 2


def near(at, i):
    return (at + (0, 3, 1, 2)[i]) % 4


def slot_scale(ranks, samples, group, slots):
    clients = slots // RMAX
    total = jnp.int32(0)
    for k in range(samples.shape[0]):
        total = total + samples[k]
    slot = lax.broadcasted_iota(jnp.int32, (1, slots), 1)
    client, m = slot // RMAX, slot % RMAX
    rank = jnp.ones((1, slots), jnp.int32)
    count = jnp.ones((1, slots), jnp.int32)
    for k in range(clients):
        rank = jnp.where(client == k, ranks[group * clients + k], rank)
        count = jnp.where(client == k, samples[group * clients + k], count)
    fraction = count.astype(jnp.float32) / jnp.full((1, slots), total, jnp.int32).astype(jnp.float32)
    scale = fraction * ALPHA / jnp.sqrt(rank.astype(jnp.float32))
    return jnp.where(m < rank, scale, jnp.float32(0.0))


def one_hot(ranks, group, slots, first, width):
    clients = slots // RMAX
    slot = lax.broadcasted_iota(jnp.int32, (1, slots), 1)
    client, m = slot // RMAX, slot % RMAX
    place = jnp.full((1, slots), -1, jnp.int32)
    start = jnp.int32(0)
    for k in range(clients):
        rank = ranks[group * clients + k]
        place = jnp.where((client == k) & (m < rank), start + m, place)
        start = start + rank
    row = lax.broadcasted_iota(jnp.int32, (width, slots), 0) + first
    return jnp.where(row == place, jnp.float32(1.0), jnp.float32(0.0)).astype(jnp.bfloat16), start


def most_live(ranks):
    def kernel(ranks_ref, out_ref):
        most = jnp.int32(0)
        for g in range(4):
            live = jnp.int32(0)
            for k in range(ranks.shape[0] // 4):
                live = live + ranks_ref[g * (ranks.shape[0] // 4) + k]
            most = jnp.maximum(most, live)
        out_ref[0] = most

    return pl.pallas_call(
        kernel,
        in_specs=[pl.BlockSpec(memory_space=pltpu.SMEM)],
        out_specs=pl.BlockSpec(memory_space=pltpu.SMEM),
        out_shape=jax.ShapeDtypeStruct((1,), jnp.int32),
        name="most_live",
    )(ranks)


def pack(up, ranks, first, width):
    rows, slots = up.shape
    half = rows // 2
    clients = slots // RMAX

    def kernel(ranks_ref, up_ref, top_ref, bottom_ref, hot):
        group = lax.axis_index("col")
        m = lax.broadcasted_iota(jnp.int32, (RMAX, width), 0)
        ahead = lax.broadcasted_iota(jnp.int32, (RMAX, width), 1) - m
        start = jnp.int32(-first)
        for k in range(clients):
            rank = ranks_ref[group * clients + k]
            here = (ahead == start) & (m < rank)
            hot[k * RMAX : (k + 1) * RMAX] = jnp.where(here, jnp.float32(1.0), jnp.float32(0.0)).astype(jnp.bfloat16)
            start = start + rank
        for j, out_ref in enumerate((top_ref, bottom_ref)):
            out_ref[...] = jnp.dot(
                up_ref[j * half : (j + 1) * half], hot[...], preferred_element_type=jnp.float32
            ).astype(jnp.bfloat16)

    return pl.pallas_call(
        kernel,
        grid_spec=pltpu.PrefetchScalarGridSpec(
            num_scalar_prefetch=1,
            grid=(1,),
            in_specs=[pl.BlockSpec(memory_space=pltpu.VMEM)],
            out_specs=[pl.BlockSpec((half, width), lambda i, *_: (0, 0))] * 2,
            scratch_shapes=[pltpu.VMEM((slots, width), jnp.bfloat16)],
        ),
        out_shape=[jax.ShapeDtypeStruct((half, width), jnp.bfloat16)] * 2,
        compiler_params=pltpu.CompilerParams(vmem_limit_bytes=VMEM_LIMIT),
        cost_estimate=pl.CostEstimate(flops=2 * rows * slots * width, bytes_accessed=4 * rows * slots, transcendentals=0),
        name="pack",
    )(ranks, pltpu.with_memory_space_constraint(up, pltpu.VMEM))


def unpack(ups, items, rest, ranks, samples, slots):
    groups = 4
    inner = slots // groups
    arrays = []
    for item in items:
        if not any(item[0] is a for a in arrays):
            arrays.append(item[0])
    index = [next(j for j, a in enumerate(arrays) if a is item[0]) for item in items]
    rows = items[0][0].shape[0] if ups is None else ups.shape[1]
    spill = slots - WIDTH
    n = len(arrays)

    def kernel(ranks_ref, samples_ref, *refs):
        part_refs, rest_ref = refs[:n], refs[n]
        out_ref, rest_v, sem = refs[-3:]

        def put(group, at, value, add):
            for z in range(groups):
                cols = slice(z * inner, (z + 1) * inner)
                target = pl.ds(pl.multiple_of(group * inner, inner), inner)
                piece = value[:, cols]
                span = slice(at, at + value.shape[0])
                if add:
                    piece = piece + out_ref[group, span, cols]
                out_ref[group, span, cols] = piece
                out_ref[groups + z, span, target] = piece

        for which in range(groups):
            mine = [(j, item) for j, item in zip(index, items) if item[2] == which]
            if not mine:
                continue
            group = near(lax.axis_index("col"), which)
            factor = slot_scale(ranks_ref, samples_ref, group, slots)
            if which > 0:
                hot, live = one_hot(ranks_ref, group, slots, 0, WIDTH)
            for j, (_, first, _, at, count) in mine:
                part = part_refs[j][first : first + count]
                if which > 0:
                    whole = jnp.dot(part, hot, preferred_element_type=jnp.float32)
                else:
                    whole = part.astype(jnp.float32)
                put(group, at, (whole * factor).astype(jnp.bfloat16), False)
            if which > 0:

                @pl.when(live > WIDTH)
                def _(mine=mine, which=which, group=group, factor=factor):
                    copy = pltpu.make_async_copy(rest_ref.at[:, (which - 1) * spill : which * spill], rest_v, sem)
                    copy.start()
                    copy.wait()
                    hot, _ = one_hot(ranks_ref, group, slots, WIDTH, spill)
                    for _, (_, _, _, at, count) in mine:
                        whole = jnp.dot(rest_v[at : at + count], hot, preferred_element_type=jnp.float32)
                        put(group, at, (whole * factor).astype(jnp.bfloat16), True)

    whole = pl.BlockSpec(memory_space=pltpu.VMEM)
    vmem = lambda a: pltpu.with_memory_space_constraint(a, pltpu.VMEM)
    extra = [] if ups is None else [vmem(ups)]
    return pl.pallas_call(
        kernel,
        grid_spec=pltpu.PrefetchScalarGridSpec(
            num_scalar_prefetch=2,
            grid=(1,),
            in_specs=[whole] * n + [pl.BlockSpec(memory_space=pl.ANY)] + [whole] * len(extra),
            out_specs=whole,
            scratch_shapes=[pltpu.VMEM((rows, spill), jnp.bfloat16), pltpu.SemaphoreType.DMA],
        ),
        out_shape=pltpu.VMEM((2 * groups, rows, slots), jnp.bfloat16),
        input_output_aliases={n + 3: 0} if extra else {},
        compiler_params=pltpu.CompilerParams(vmem_limit_bytes=VMEM_LIMIT),
        cost_estimate=pl.CostEstimate(flops=UNPACK_FLOPS, bytes_accessed=6 * rows * slots, transcendentals=0),
        name="unpack",
    )(ranks, samples, *[vmem(a) for a in arrays], rest, *extra)


def pick(mine, other):
    rows, columns = mine.shape

    def kernel(mine_ref, other_ref, out_ref):
        core = lax.axis_index("row") % 2
        for n in range(columns // 2 // CHUNK):
            cols = slice(n * CHUNK, (n + 1) * CHUNK)
            out_ref[n, pl.ds(pl.multiple_of(core * rows, rows), rows)] = mine_ref[:, cols]
            out_ref[n, pl.ds(pl.multiple_of((1 - core) * rows, rows), rows)] = other_ref[:, cols]

    return pl.pallas_call(
        kernel,
        grid=(1,),
        in_specs=[pl.BlockSpec((rows, columns // 2), lambda i: (0, lax.axis_index("row") % 2))] * 2,
        out_specs=pl.BlockSpec((columns // 2 // CHUNK, 2 * rows, CHUNK), lambda i: (0, 0, 0)),
        out_shape=jax.ShapeDtypeStruct((columns // 2 // CHUNK, 2 * rows, CHUNK), mine.dtype),
        compiler_params=pltpu.CompilerParams(vmem_limit_bytes=VMEM_LIMIT),
        cost_estimate=pl.CostEstimate(flops=0, bytes_accessed=4 * rows * columns, transcendentals=0),
        name="pick",
    )(mine, other)


def halves(upper_of, lower_of):
    chunks, rows, columns = upper_of.shape
    half = rows // 2

    def kernel(a_ref, b_ref, upper_ref, lower_ref, sem):
        copies = [
            pltpu.make_async_copy(a_ref.at[:, pl.ds(0, half)], upper_ref, sem.at[0]),
            pltpu.make_async_copy(b_ref.at[:, pl.ds(half, half)], lower_ref, sem.at[1]),
        ]
        for copy in copies:
            copy.start()
        for copy in copies:
            copy.wait()

    return pl.pallas_call(
        kernel,
        in_specs=[pl.BlockSpec(memory_space=pl.ANY)] * 2,
        out_specs=[pl.BlockSpec(memory_space=pl.ANY)] * 2,
        out_shape=[jax.ShapeDtypeStruct((chunks, half, columns), upper_of.dtype)] * 2,
        scratch_shapes=[pltpu.SemaphoreType.DMA((2,))],
        compiler_params=pltpu.CompilerParams(vmem_limit_bytes=VMEM_LIMIT),
        cost_estimate=pl.CostEstimate(flops=0, bytes_accessed=4 * rows * columns, transcendentals=0),
        name="halves",
    )(upper_of, lower_of)


def line_up(pieces):
    chunks, rows, columns = pieces[0].shape

    def kernel(*refs):
        x, z, core = torus_place()
        at = jnp.where(core == 0, x, z)
        for i in range(4):
            refs[4][:, pl.ds(pl.multiple_of(near(at, (3, 1, 2, 0)[i]) * rows, rows), rows)] = refs[i][...]

    return pl.pallas_call(
        kernel,
        out_shape=jax.ShapeDtypeStruct((chunks, 4 * rows, columns), pieces[0].dtype),
        compiler_params=pltpu.CompilerParams(vmem_limit_bytes=VMEM_LIMIT),
        cost_estimate=pl.CostEstimate(flops=0, bytes_accessed=16 * chunks * rows * columns, transcendentals=0),
        name="line_up",
    )(*pieces)


def merge(ups, lines, base, theirs, at, width):
    _, rows, slots = ups.shape
    part = rows // 4
    features = base.shape[1]

    def half():
        core = lax.axis_index("row") % 2
        return 1 - core if theirs else core

    def kernel(ups_ref, l0, l1, l2, l3, l4, base_ref, o0, o1, o2, o3, d_v, base_v, total, d_sem, base_sem):
        x, z, _ = torus_place()
        core = half()
        along = jnp.where(core == 0, z, x)
        first = jnp.where(core == 0, 4, 0)
        where = ((l0, slots), (l1, slots), (l2, slots), (l3, slots // 2), (l4, slots // 2))
        copies = []
        row = 0
        for j, (line, count) in enumerate(where):
            copies.append(pltpu.make_async_copy(line.at[at // width], d_v.at[pl.ds(row, count)], d_sem.at[j]))
            row += count
        base_at = pl.ds(pl.multiple_of(half() * (features // 2) + at, width), width)
        copies.append(pltpu.make_async_copy(base_ref.at[:, base_at], base_v, base_sem))
        for copy in copies:
            copy.start()
        for i in range(4):
            for copy in copies[i:] if i == 3 else copies[i : i + 1]:
                copy.wait()
            product = jnp.dot(
                ups_ref[first + near(along, i)], d_v[i * slots : (i + 1) * slots], preferred_element_type=jnp.float32
            )
            if i == 0:
                total[...] = product
            else:
                total[...] += product
        col = lax.axis_index("col")
        for i, out in enumerate((o0, o1, o2, o3)):
            r = pl.ds(pl.multiple_of(near(col, i) * part, 32), part)
            out[...] = (base_v[r, :].astype(jnp.float32) + total[r, :]).astype(jnp.bfloat16)

    hold = pl.BlockSpec(memory_space=pl.ANY)
    return pl.pallas_call(
        kernel,
        grid=(1,),
        in_specs=[pl.BlockSpec(memory_space=pltpu.VMEM)] + [hold] * 6,
        out_specs=[pl.BlockSpec((part, width), lambda i: (0, 0))] * 4,
        scratch_shapes=[
            pltpu.VMEM((4 * slots, width), jnp.bfloat16),
            pltpu.VMEM((rows, width), jnp.bfloat16),
            pltpu.VMEM((rows, width), jnp.float32),
            pltpu.SemaphoreType.DMA((5,)),
            pltpu.SemaphoreType.DMA,
        ],
        out_shape=[jax.ShapeDtypeStruct((part, width), jnp.bfloat16)] * 4,
        compiler_params=pltpu.CompilerParams(vmem_limit_bytes=MERGE_LIMIT),
        cost_estimate=pl.CostEstimate(flops=2 * rows * 4 * slots * width, bytes_accessed=4 * rows * width, transcendentals=0),
        name="merge",
    )(pltpu.with_memory_space_constraint(ups, pltpu.VMEM), *lines, base)


def place(out, pieces, chunk, features):
    part, width = pieces[0].shape
    theirs, at = chunk

    def block(n):
        core = lax.axis_index("row") % 2
        half = 1 - core if theirs else core
        return n * (features // 4 // width) + half * (features // 8 // width) + at // width

    def kernel(*refs):
        for i in range(4):

            @pl.when(near(lax.axis_index("col"), (3, 1, 2, 0)[i]) == pl.program_id(0))
            def _(i=i):
                refs[-1][...] = refs[i][...]

    extra = [] if out is None else [out]
    return pl.pallas_call(
        kernel,
        grid=(4,),
        in_specs=[pl.BlockSpec((part, width), lambda n: (0, 0))] * 4 + [pl.BlockSpec(memory_space=pl.ANY)] * len(extra),
        out_specs=pl.BlockSpec((part, width), lambda n: (0, block(n))),
        out_shape=jax.ShapeDtypeStruct((part, features), jnp.bfloat16),
        input_output_aliases={4: 0} if extra else {},
        compiler_params=pltpu.CompilerParams(vmem_limit_bytes=VMEM_LIMIT),
        cost_estimate=pl.CostEstimate(flops=0, bytes_accessed=16 * part * width, transcendentals=0),
        name="place",
    )(*pieces, *extra)


def ring(step):
    return [(i, (i + step) % 4) for i in range(4)]


def torus(step, first):
    pairs = []
    for x in range(4):
        for z in range(4):
            for core in range(2):
                along_x = (core == 0) == first
                to = ((x + step) % 4, z) if along_x else (x, (z + step) % 4)
                pairs.append(((x * 4 + z) * 2 + core, (to[0] * 4 + to[1]) * 2 + core))
    return pairs


SWAP = [(i, i ^ 1) for i in range(32)]


def after(value, *others):
    return lax.optimization_barrier((value, *others))[0]


def shards(base, down, up, ranks, samples):
    rows, slots = up.shape
    features = base.shape[1]

    half = rows // 2
    top, bottom = pack(up, ranks, 0, WIDTH)
    mine = pick(down, lax.ppermute(down, "row", SWAP))
    mine, top, bottom = lax.optimization_barrier((mine, top, bottom))

    left_top = lax.ppermute(top, "col", ring(1))
    right_bottom = lax.ppermute(bottom, "col", ring(3))
    def send_rest(up, ranks):
        own = jnp.concatenate(pack(up, ranks, WIDTH, slots - WIDTH))
        return jnp.concatenate([lax.ppermute(own, "col", ring(k)) for k in (1, 3, 2)], axis=1)

    def no_rest(up, ranks):
        return jnp.zeros((rows, 3 * (slots - WIDTH)), jnp.bfloat16)

    rest = lax.cond(most_live(ranks)[0] > WIDTH, send_rest, no_rest, up, ranks)
    ups = unpack(None, [(up, 0, 0, 0, rows)], rest, ranks, samples, slots)
    mine, ups = lax.optimization_barrier((mine, ups))
    piece_far = lax.ppermute(mine, "row", torus(2, True))
    piece_left = lax.ppermute(mine, "row", torus(1, True))
    piece_right = lax.ppermute(mine, "row", torus(3, True))
    piece_far, piece_left, piece_right, mine, left_top, right_bottom, top, bottom, ups = lax.optimization_barrier(
        (piece_far, piece_left, piece_right, mine, left_top, right_bottom, top, bottom, ups)
    )

    line = line_up([piece_far, piece_left, piece_right, mine])
    line_left = lax.ppermute(line, "row", torus(1, False))
    line_right = lax.ppermute(line, "row", torus(3, False))
    from_left = lax.ppermute(jnp.concatenate([bottom, left_top[:EARLY]]), "col", ring(1))
    from_right = lax.ppermute(jnp.concatenate([top, right_bottom[:EARLY]]), "col", ring(3))
    line_there = lax.ppermute(line, "row", SWAP)
    ups = unpack(ups, [(left_top, 0, 1, 0, half), (right_bottom, 0, 2, half, half)], rest, ranks, samples, slots)
    line, line_left, line_right, from_left, from_right, line_there, left_top, right_bottom, ups = (
        lax.optimization_barrier(
            (line, line_left, line_right, from_left, from_right, line_there, left_top, right_bottom, ups)
        )
    )

    upper, lower = halves(line_left, line_right)
    line_far = [lax.ppermute(upper, "row", torus(1, False)), lax.ppermute(lower, "row", torus(3, False))]
    late_left = lax.ppermute(left_top[EARLY:], "col", ring(1))
    late_right = lax.ppermute(right_bottom[EARLY:], "col", ring(3))
    left_there = lax.ppermute(line_left, "row", SWAP)
    ups = unpack(
        ups,
        [
            (from_left, 0, 1, half, half),
            (from_right, 0, 2, 0, half),
            (from_left, half, 3, 0, EARLY),
            (from_right, half, 3, half, EARLY),
        ],
        rest, ranks, samples, slots,
    )
    *line_far, late_left, late_right, left_there, ups = lax.optimization_barrier(
        (*line_far, late_left, late_right, left_there, ups)
    )
    ups = unpack(
        ups,
        [(late_left, 0, 3, EARLY, half - EARLY), (late_right, 0, 3, half + EARLY, half - EARLY)],
        rest, ranks, samples, slots,
    )
    lines = [line, line_left, line_right, *line_far]
    other_lines = [line_there, left_there] + [lax.ppermute(a, "row", SWAP) for a in lines[2:]]

    out, first = None, True
    for theirs, from_lines in ((False, lines), (True, other_lines)):
        for at, width in CHUNKS[theirs]:
            if not first and not theirs:
                ups, *other_lines[2:] = lax.optimization_barrier((ups, *other_lines[2:]))
            first = False
            own, to_left, to_right, to_far = merge(ups, from_lines, base, theirs, at, width)
            from_far = lax.ppermute(to_far, "col", ring(2))
            from_left = lax.ppermute(to_right, "col", ring(1))
            from_right = lax.ppermute(to_left, "col", ring(3))
            out = place(out, [from_far, from_left, from_right, own], (theirs, at), 4 * features)
    return out


def solution(mesh):
    placed = (P("row", "col"), P("row", "col"), P("row", "col"), P(), P())
    return jax.shard_map(
        shards, mesh=mesh, in_specs=placed, out_specs=P(("row", "col"), None), check_vma=False
    )
```

```python
import jax
import jax.numpy as jnp
from jax import lax
from jax.experimental import pallas as pl
from jax.experimental.pallas import tpu as pltpu
from jax.sharding import PartitionSpec as P

RMAX = 64
ALPHA = 8.0
WIDTH = 768
CHUNK = 512
CHUNKS = (((0, 512), (512, 512)), ((0, 512), (512, 512)))
VMEM_LIMIT = 12 * 2**20
EARLY = 176
UNPACK_FLOPS = 30 * 10**9
MERGE_LIMIT = 22 * 2**20


def torus_place():
    row = lax.axis_index("row")
    return row // 8, (row // 2) % 4, row % 2


def near(at, i):
    return (at + (0, 3, 1, 2)[i]) % 4


def slot_scale(ranks, samples, group, slots):
    clients = slots // RMAX
    total = jnp.int32(0)
    for k in range(samples.shape[0]):
        total = total + samples[k]
    slot = lax.broadcasted_iota(jnp.int32, (1, slots), 1)
    client, m = slot // RMAX, slot % RMAX
    rank = jnp.ones((1, slots), jnp.int32)
    count = jnp.ones((1, slots), jnp.int32)
    for k in range(clients):
        rank = jnp.where(client == k, ranks[group * clients + k], rank)
        count = jnp.where(client == k, samples[group * clients + k], count)
    fraction = count.astype(jnp.float32) / jnp.full((1, slots), total, jnp.int32).astype(jnp.float32)
    scale = fraction * ALPHA / jnp.sqrt(rank.astype(jnp.float32))
    return jnp.where(m < rank, scale, jnp.float32(0.0))


def one_hot(ranks, group, slots, first, width):
    clients = slots // RMAX
    slot = lax.broadcasted_iota(jnp.int32, (1, slots), 1)
    client, m = slot // RMAX, slot % RMAX
    place = jnp.full((1, slots), -1, jnp.int32)
    start = jnp.int32(0)
    for k in range(clients):
        rank = ranks[group * clients + k]
        place = jnp.where((client == k) & (m < rank), start + m, place)
        start = start + rank
    row = lax.broadcasted_iota(jnp.int32, (width, slots), 0) + first
    return jnp.where(row == place, jnp.float32(1.0), jnp.float32(0.0)).astype(jnp.bfloat16), start


def most_live(ranks):
    def kernel(ranks_ref, out_ref):
        most = jnp.int32(0)
        for g in range(4):
            live = jnp.int32(0)
            for k in range(ranks.shape[0] // 4):
                live = live + ranks_ref[g * (ranks.shape[0] // 4) + k]
            most = jnp.maximum(most, live)
        out_ref[0] = most

    return pl.pallas_call(
        kernel,
        in_specs=[pl.BlockSpec(memory_space=pltpu.SMEM)],
        out_specs=pl.BlockSpec(memory_space=pltpu.SMEM),
        out_shape=jax.ShapeDtypeStruct((1,), jnp.int32),
        name="most_live",
    )(ranks)


def pack(up, ranks, first, width):
    rows, slots = up.shape
    half = rows // 2
    clients = slots // RMAX

    def kernel(ranks_ref, up_ref, top_ref, bottom_ref, hot):
        group = lax.axis_index("col")
        m = lax.broadcasted_iota(jnp.int32, (RMAX, width), 0)
        ahead = lax.broadcasted_iota(jnp.int32, (RMAX, width), 1) - m
        start = jnp.int32(-first)
        for k in range(clients):
            rank = ranks_ref[group * clients + k]
            here = (ahead == start) & (m < rank)
            hot[k * RMAX : (k + 1) * RMAX] = jnp.where(here, jnp.float32(1.0), jnp.float32(0.0)).astype(jnp.bfloat16)
            start = start + rank
        for j, out_ref in enumerate((top_ref, bottom_ref)):
            out_ref[...] = jnp.dot(
                up_ref[j * half : (j + 1) * half], hot[...], preferred_element_type=jnp.float32
            ).astype(jnp.bfloat16)

    return pl.pallas_call(
        kernel,
        grid_spec=pltpu.PrefetchScalarGridSpec(
            num_scalar_prefetch=1,
            grid=(1,),
            in_specs=[pl.BlockSpec(memory_space=pltpu.VMEM)],
            out_specs=[pl.BlockSpec((half, width), lambda i, *_: (0, 0))] * 2,
            scratch_shapes=[pltpu.VMEM((slots, width), jnp.bfloat16)],
        ),
        out_shape=[jax.ShapeDtypeStruct((half, width), jnp.bfloat16)] * 2,
        compiler_params=pltpu.CompilerParams(vmem_limit_bytes=VMEM_LIMIT),
        cost_estimate=pl.CostEstimate(flops=2 * rows * slots * width, bytes_accessed=4 * rows * slots, transcendentals=0),
        name="pack",
    )(ranks, pltpu.with_memory_space_constraint(up, pltpu.VMEM))


def unpack(ups, items, rest, ranks, samples, slots):
    groups = 4
    inner = slots // groups
    arrays = []
    for item in items:
        if not any(item[0] is a for a in arrays):
            arrays.append(item[0])
    index = [next(j for j, a in enumerate(arrays) if a is item[0]) for item in items]
    rows = items[0][0].shape[0] if ups is None else ups.shape[1]
    spill = slots - WIDTH
    n = len(arrays)

    def kernel(ranks_ref, samples_ref, *refs):
        part_refs, rest_ref = refs[:n], refs[n]
        out_ref, rest_v, sem = refs[-3:]

        def put(group, at, value, add):
            for z in range(groups):
                cols = slice(z * inner, (z + 1) * inner)
                target = pl.ds(pl.multiple_of(group * inner, inner), inner)
                piece = value[:, cols]
                span = slice(at, at + value.shape[0])
                if add:
                    piece = piece + out_ref[group, span, cols]
                out_ref[group, span, cols] = piece
                out_ref[groups + z, span, target] = piece

        for which in range(groups):
            mine = [(j, item) for j, item in zip(index, items) if item[2] == which]
            if not mine:
                continue
            group = near(lax.axis_index("col"), which)
            factor = slot_scale(ranks_ref, samples_ref, group, slots)
            if which > 0:
                hot, live = one_hot(ranks_ref, group, slots, 0, WIDTH)
            for j, (_, first, _, at, count) in mine:
                part = part_refs[j][first : first + count]
                if which > 0:
                    whole = jnp.dot(part, hot, preferred_element_type=jnp.float32)
                else:
                    whole = part.astype(jnp.float32)
                put(group, at, (whole * factor).astype(jnp.bfloat16), False)
            if which > 0:

                @pl.when(live > WIDTH)
                def _(mine=mine, which=which, group=group, factor=factor):
                    copy = pltpu.make_async_copy(rest_ref.at[:, (which - 1) * spill : which * spill], rest_v, sem)
                    copy.start()
                    copy.wait()
                    hot, _ = one_hot(ranks_ref, group, slots, WIDTH, spill)
                    for _, (_, _, _, at, count) in mine:
                        whole = jnp.dot(rest_v[at : at + count], hot, preferred_element_type=jnp.float32)
                        put(group, at, (whole * factor).astype(jnp.bfloat16), True)

    whole = pl.BlockSpec(memory_space=pltpu.VMEM)
    vmem = lambda a: pltpu.with_memory_space_constraint(a, pltpu.VMEM)
    extra = [] if ups is None else [vmem(ups)]
    return pl.pallas_call(
        kernel,
        grid_spec=pltpu.PrefetchScalarGridSpec(
            num_scalar_prefetch=2,
            grid=(1,),
            in_specs=[whole] * n + [pl.BlockSpec(memory_space=pl.ANY)] + [whole] * len(extra),
            out_specs=whole,
            scratch_shapes=[pltpu.VMEM((rows, spill), jnp.bfloat16), pltpu.SemaphoreType.DMA],
        ),
        out_shape=pltpu.VMEM((2 * groups, rows, slots), jnp.bfloat16),
        input_output_aliases={n + 3: 0} if extra else {},
        compiler_params=pltpu.CompilerParams(vmem_limit_bytes=VMEM_LIMIT),
        cost_estimate=pl.CostEstimate(flops=UNPACK_FLOPS, bytes_accessed=6 * rows * slots, transcendentals=0),
        name="unpack",
    )(ranks, samples, *[vmem(a) for a in arrays], rest, *extra)


def pick(mine, other):
    rows, columns = mine.shape

    def kernel(mine_ref, other_ref, out_ref):
        core = lax.axis_index("row") % 2
        for n in range(columns // 2 // CHUNK):
            cols = slice(n * CHUNK, (n + 1) * CHUNK)
            out_ref[n, pl.ds(pl.multiple_of(core * rows, rows), rows)] = mine_ref[:, cols]
            out_ref[n, pl.ds(pl.multiple_of((1 - core) * rows, rows), rows)] = other_ref[:, cols]

    return pl.pallas_call(
        kernel,
        grid=(1,),
        in_specs=[pl.BlockSpec((rows, columns // 2), lambda i: (0, lax.axis_index("row") % 2))] * 2,
        out_specs=pl.BlockSpec((columns // 2 // CHUNK, 2 * rows, CHUNK), lambda i: (0, 0, 0)),
        out_shape=jax.ShapeDtypeStruct((columns // 2 // CHUNK, 2 * rows, CHUNK), mine.dtype),
        compiler_params=pltpu.CompilerParams(vmem_limit_bytes=VMEM_LIMIT),
        cost_estimate=pl.CostEstimate(flops=0, bytes_accessed=4 * rows * columns, transcendentals=0),
        name="pick",
    )(mine, other)


def halves(upper_of, lower_of):
    chunks, rows, columns = upper_of.shape
    half = rows // 2

    def kernel(a_ref, b_ref, upper_ref, lower_ref, sem):
        copies = [
            pltpu.make_async_copy(a_ref.at[:, pl.ds(0, half)], upper_ref, sem.at[0]),
            pltpu.make_async_copy(b_ref.at[:, pl.ds(half, half)], lower_ref, sem.at[1]),
        ]
        for copy in copies:
            copy.start()
        for copy in copies:
            copy.wait()

    return pl.pallas_call(
        kernel,
        in_specs=[pl.BlockSpec(memory_space=pl.ANY)] * 2,
        out_specs=[pl.BlockSpec(memory_space=pl.ANY)] * 2,
        out_shape=[jax.ShapeDtypeStruct((chunks, half, columns), upper_of.dtype)] * 2,
        scratch_shapes=[pltpu.SemaphoreType.DMA((2,))],
        compiler_params=pltpu.CompilerParams(vmem_limit_bytes=VMEM_LIMIT),
        cost_estimate=pl.CostEstimate(flops=0, bytes_accessed=4 * rows * columns, transcendentals=0),
        name="halves",
    )(upper_of, lower_of)


def line_up(pieces):
    chunks, rows, columns = pieces[0].shape

    def kernel(*refs):
        x, z, core = torus_place()
        at = jnp.where(core == 0, x, z)
        for i in range(4):
            refs[4][:, pl.ds(pl.multiple_of(near(at, (3, 1, 2, 0)[i]) * rows, rows), rows)] = refs[i][...]

    return pl.pallas_call(
        kernel,
        out_shape=jax.ShapeDtypeStruct((chunks, 4 * rows, columns), pieces[0].dtype),
        compiler_params=pltpu.CompilerParams(vmem_limit_bytes=VMEM_LIMIT),
        cost_estimate=pl.CostEstimate(flops=0, bytes_accessed=16 * chunks * rows * columns, transcendentals=0),
        name="line_up",
    )(*pieces)


def merge(ups, lines, base, theirs, at, width):
    _, rows, slots = ups.shape
    part = rows // 4
    features = base.shape[1]

    def half():
        core = lax.axis_index("row") % 2
        return 1 - core if theirs else core

    def kernel(ups_ref, l0, l1, l2, l3, l4, base_ref, o0, o1, o2, o3, d_v, base_v, total, d_sem, base_sem):
        x, z, _ = torus_place()
        core = half()
        along = jnp.where(core == 0, z, x)
        first = jnp.where(core == 0, 4, 0)
        where = ((l0, slots), (l1, slots), (l2, slots), (l3, slots // 2), (l4, slots // 2))
        copies = []
        row = 0
        for j, (line, count) in enumerate(where):
            copies.append(pltpu.make_async_copy(line.at[at // width], d_v.at[pl.ds(row, count)], d_sem.at[j]))
            row += count
        base_at = pl.ds(pl.multiple_of(half() * (features // 2) + at, width), width)
        copies.append(pltpu.make_async_copy(base_ref.at[:, base_at], base_v, base_sem))
        for copy in copies:
            copy.start()
        for i in range(4):
            for copy in copies[i:] if i == 3 else copies[i : i + 1]:
                copy.wait()
            product = jnp.dot(
                ups_ref[first + near(along, i)], d_v[i * slots : (i + 1) * slots], preferred_element_type=jnp.float32
            )
            if i == 0:
                total[...] = product
            else:
                total[...] += product
        col = lax.axis_index("col")
        for i, out in enumerate((o0, o1, o2, o3)):
            r = pl.ds(pl.multiple_of(near(col, i) * part, 32), part)
            out[...] = (base_v[r, :].astype(jnp.float32) + total[r, :]).astype(jnp.bfloat16)

    hold = pl.BlockSpec(memory_space=pl.ANY)
    return pl.pallas_call(
        kernel,
        grid=(1,),
        in_specs=[pl.BlockSpec(memory_space=pltpu.VMEM)] + [hold] * 6,
        out_specs=[pl.BlockSpec((part, width), lambda i: (0, 0))] * 4,
        scratch_shapes=[
            pltpu.VMEM((4 * slots, width), jnp.bfloat16),
            pltpu.VMEM((rows, width), jnp.bfloat16),
            pltpu.VMEM((rows, width), jnp.float32),
            pltpu.SemaphoreType.DMA((5,)),
            pltpu.SemaphoreType.DMA,
        ],
        out_shape=[jax.ShapeDtypeStruct((part, width), jnp.bfloat16)] * 4,
        compiler_params=pltpu.CompilerParams(vmem_limit_bytes=MERGE_LIMIT),
        cost_estimate=pl.CostEstimate(flops=2 * rows * 4 * slots * width, bytes_accessed=4 * rows * width, transcendentals=0),
        name="merge",
    )(pltpu.with_memory_space_constraint(ups, pltpu.VMEM), *lines, base)


def place(out, pieces, chunk, features):
    part, width = pieces[0].shape
    theirs, at = chunk

    def kernel(*refs):
        out_ref, sem = refs[-2:]
        core = lax.axis_index("row") % 2
        half = 1 - core if theirs else core
        copies = []
        for i in range(4):
            owner = near(lax.axis_index("col"), (3, 1, 2, 0)[i])
            start = owner * (features // 4) + half * (features // 8) + at
            cols = pl.ds(pl.multiple_of(start, width), width)
            copies.append(pltpu.make_async_copy(refs[i], out_ref.at[:, cols], sem.at[i]))
            copies[-1].start()
        for copy in copies:
            copy.wait()

    extra = [] if out is None else [out]
    return pl.pallas_call(
        kernel,
        in_specs=[pl.BlockSpec(memory_space=pltpu.VMEM)] * 4 + [pl.BlockSpec(memory_space=pl.ANY)] * len(extra),
        out_specs=pl.BlockSpec(memory_space=pl.ANY),
        out_shape=jax.ShapeDtypeStruct((part, features), jnp.bfloat16),
        scratch_shapes=[pltpu.SemaphoreType.DMA((4,))],
        input_output_aliases={4: 0} if extra else {},
        compiler_params=pltpu.CompilerParams(vmem_limit_bytes=VMEM_LIMIT),
        cost_estimate=pl.CostEstimate(flops=0, bytes_accessed=16 * part * width, transcendentals=0),
        name="place",
    )(*[pltpu.with_memory_space_constraint(a, pltpu.VMEM) for a in pieces], *extra)


def ring(step):
    return [(i, (i + step) % 4) for i in range(4)]


def torus(step, first):
    pairs = []
    for x in range(4):
        for z in range(4):
            for core in range(2):
                along_x = (core == 0) == first
                to = ((x + step) % 4, z) if along_x else (x, (z + step) % 4)
                pairs.append(((x * 4 + z) * 2 + core, (to[0] * 4 + to[1]) * 2 + core))
    return pairs


SWAP = [(i, i ^ 1) for i in range(32)]


def after(value, *others):
    return lax.optimization_barrier((value, *others))[0]


def shards(base, down, up, ranks, samples):
    rows, slots = up.shape
    features = base.shape[1]

    half = rows // 2
    top, bottom = pack(up, ranks, 0, WIDTH)
    mine = pick(down, lax.ppermute(down, "row", SWAP))
    mine, top, bottom = lax.optimization_barrier((mine, top, bottom))

    left_top = lax.ppermute(top, "col", ring(1))
    right_bottom = lax.ppermute(bottom, "col", ring(3))
    def send_rest(up, ranks):
        own = jnp.concatenate(pack(up, ranks, WIDTH, slots - WIDTH))
        return jnp.concatenate([lax.ppermute(own, "col", ring(k)) for k in (1, 3, 2)], axis=1)

    def no_rest(up, ranks):
        return jnp.zeros((rows, 3 * (slots - WIDTH)), jnp.bfloat16)

    rest = lax.cond(most_live(ranks)[0] > WIDTH, send_rest, no_rest, up, ranks)
    ups = unpack(None, [(up, 0, 0, 0, rows)], rest, ranks, samples, slots)
    mine, ups = lax.optimization_barrier((mine, ups))
    piece_far = lax.ppermute(mine, "row", torus(2, True))
    piece_left = lax.ppermute(mine, "row", torus(1, True))
    piece_right = lax.ppermute(mine, "row", torus(3, True))
    piece_far, piece_left, piece_right, mine, left_top, right_bottom, top, bottom, ups = lax.optimization_barrier(
        (piece_far, piece_left, piece_right, mine, left_top, right_bottom, top, bottom, ups)
    )

    line = line_up([piece_far, piece_left, piece_right, mine])
    line_left = lax.ppermute(line, "row", torus(1, False))
    line_right = lax.ppermute(line, "row", torus(3, False))
    from_left = lax.ppermute(jnp.concatenate([bottom, left_top[:EARLY]]), "col", ring(1))
    from_right = lax.ppermute(jnp.concatenate([top, right_bottom[:EARLY]]), "col", ring(3))
    line_there = lax.ppermute(line, "row", SWAP)
    ups = unpack(ups, [(left_top, 0, 1, 0, half), (right_bottom, 0, 2, half, half)], rest, ranks, samples, slots)
    line, line_left, line_right, from_left, from_right, line_there, left_top, right_bottom, ups = (
        lax.optimization_barrier(
            (line, line_left, line_right, from_left, from_right, line_there, left_top, right_bottom, ups)
        )
    )

    upper, lower = halves(line_left, line_right)
    line_far = [lax.ppermute(upper, "row", torus(1, False)), lax.ppermute(lower, "row", torus(3, False))]
    late_left = lax.ppermute(left_top[EARLY:], "col", ring(1))
    late_right = lax.ppermute(right_bottom[EARLY:], "col", ring(3))
    left_there = lax.ppermute(line_left, "row", SWAP)
    ups = unpack(
        ups,
        [
            (from_left, 0, 1, half, half),
            (from_right, 0, 2, 0, half),
            (from_left, half, 3, 0, EARLY),
            (from_right, half, 3, half, EARLY),
        ],
        rest, ranks, samples, slots,
    )
    *line_far, late_left, late_right, left_there, ups = lax.optimization_barrier(
        (*line_far, late_left, late_right, left_there, ups)
    )
    ups = unpack(
        ups,
        [(late_left, 0, 3, EARLY, half - EARLY), (late_right, 0, 3, half + EARLY, half - EARLY)],
        rest, ranks, samples, slots,
    )
    lines = [line, line_left, line_right, *line_far]
    other_lines = [line_there, left_there] + [lax.ppermute(a, "row", SWAP) for a in lines[2:]]

    out, first = None, True
    for theirs, from_lines in ((False, lines), (True, other_lines)):
        for at, width in CHUNKS[theirs]:
            if not first and not theirs:
                ups, *other_lines[2:] = lax.optimization_barrier((ups, *other_lines[2:]))
            first = False
            own, to_left, to_right, to_far = merge(ups, from_lines, base, theirs, at, width)
            from_far = lax.ppermute(to_far, "col", ring(2))
            from_left = lax.ppermute(to_right, "col", ring(1))
            from_right = lax.ppermute(to_left, "col", ring(3))
            out = place(out, [from_far, from_left, from_right, own], (theirs, at), 4 * features)
    return out


def solution(mesh):
    placed = (P("row", "col"), P("row", "col"), P("row", "col"), P(), P())
    return jax.shard_map(
        shards, mesh=mesh, in_specs=placed, out_specs=P(("row", "col"), None), check_vma=False
    )
```
